32 devices in a mesh: seq: 8 (over z, x), head: 4 (over y, core).
Axes of the slice: x: 2, y: 2, z: 4, core: 2. Of those that a mesh axis runs over, the one named last changes fastest.
Arguments:
- queries: bfloat16 [8192, 4096], P(('seq', 'head')), may hold values from -10 to 10
- key_rows: bfloat16 [8192, 4096], P(('seq', 'head')), may hold values from -10 to 10
- value_rows: bfloat16 [8192, 4096], P(('seq', 'head')), may hold values from -6 to 6
- cotangent: bfloat16 [8192, 4096], P(('seq', 'head')), may hold values from -6 to 6
- neighbours: int32 [64, 8], replicated, may hold values from 0 to 63, as said below
- counts: int32 [64], replicated, may hold values from 2 to 8, as said below
Outputs:
- attended: bfloat16 [8192, 4096], P(('seq', 'head'))
- grad_queries: bfloat16 [8192, 4096], P(('seq', 'head'))
- grad_keys: bfloat16 [8192, 4096], P(('seq', 'head'))
- grad_values: bfloat16 [8192, 4096], P(('seq', 'head'))
The draws below stay inside these ranges and needn't reach their ends.
Inputs may be any that keep to these rules, and one draw needn't show every extreme that they name: `neighbours`: row b holds 8 different block numbers: the first is b, the second is b + 8 modulo 64 for even b and b - 8 modulo 64 for odd b, every other is b + o modulo 64 with 1 <= |o| <= 8. Only the first counts[b] slots of row b are used; some block uses all and some uses 2.
All inputs are finite; a program needn't handle non-finite values.
Results may differ from the reference program's by a relative error of at most 0.025.
Values may be sent and summed in bfloat16 or wider, within the bound.
A program may use at most 192 MiB of HBM per device.

```python
import jax
import jax.numpy as jnp
from jax import lax

HEADS = 32
HEAD_DIM = 128
BLOCK = 128
NB = 8
BLK_DEV = 8
WIDTH = 4096
NBLK = 64
TOKENS = 8192


def drawn_pair(key):
    width = HEADS * HEAD_DIM
    base_key = jax.random.fold_in(key, 7)
    query_rows = jnp.clip(jax.random.normal(jax.random.fold_in(base_key, 4), (TOKENS, width), jnp.float32), -6.0, 6.0)
    key_rows = jnp.clip(jax.random.normal(jax.random.fold_in(base_key, 5), (TOKENS, width), jnp.float32), -6.0, 6.0)
    return (query_rows, key_rows)


def draw_queries(key, part):
    return drawn_pair(key)[0].astype(jnp.bfloat16)


def draw_key_rows(key, part):
    return drawn_pair(key)[1].astype(jnp.bfloat16)


def draw_neighbours(key, part):
    key = jax.random.fold_in(key, 11)
    span_width = 2 * BLK_DEV
    block_ids = jnp.arange(NBLK, dtype=jnp.int32)
    upward = block_ids % 2 == 0
    fixed_column = jnp.where(upward, span_width - 1, 0).astype(jnp.int32)
    columns = jnp.arange(span_width, dtype=jnp.int32)[None, :]
    scores = jax.random.randint(key, (NBLK, span_width), 0, 2 ** 20) * span_width + columns
    scores = jnp.where(columns == fixed_column[:, None], 2 ** 30, scores)
    ranking = jnp.argsort(scores, axis=1)[:, :NB - 2].astype(jnp.int32)
    offsets = jnp.where(ranking < BLK_DEV, ranking - BLK_DEV, ranking - BLK_DEV + 1)
    second = jnp.where(upward, BLK_DEV, -BLK_DEV).astype(jnp.int32)[:, None]
    offsets = jnp.concatenate((jnp.zeros((NBLK, 1), jnp.int32), second, offsets.astype(jnp.int32)), axis=1)
    return ((block_ids[:, None] + offsets) % NBLK).astype(jnp.int32)


def draw_counts(key, part):
    drawn = jax.random.randint(jax.random.fold_in(key, 1), (NBLK,), 2, NB + 1)
    fullest = jax.random.randint(jax.random.fold_in(key, 2), (), 0, NBLK)
    emptiest = (fullest + 1 + jax.random.randint(jax.random.fold_in(key, 3), (), 0, NBLK - 1)) % NBLK
    drawn = drawn.at[fullest].set(NB).at[emptiest].set(2)
    return drawn.astype(jnp.int32)


def block_scale(rng, shape, shards, low, largest):
    gain = 1.0
    for axis_at, blocks in shards:
        heights = jax.random.uniform(jax.random.fold_in(jax.random.fold_in(rng, 6), axis_at), (blocks,), jnp.float32, low / len(shards), largest / len(shards))
        gain = gain * jnp.repeat(jnp.exp(heights), shape[axis_at] // blocks).reshape((-1,) + (1,) * (len(shape) - 1 - axis_at))
    return gain


def scatter_about(stream_key, shape, scale, most, cuts=(), kind=jnp.bfloat16):
    values = scale * jax.random.normal(stream_key, shape, jnp.float32)
    if cuts:
        values = values * block_scale(stream_key, shape, cuts, -0.22, 0.18)
    return jnp.clip(values, -most, most).astype(kind)


def setup_inputs(seed: int = 0) -> dict:
    splits = jax.random.split(jax.random.key(seed), 7)
    queries = draw_queries(jax.random.fold_in(splits[6], 71), 0)
    key_rows = draw_key_rows(jax.random.fold_in(splits[6], 71), 0)
    value_rows = scatter_about(splits[2], (TOKENS, WIDTH), 1.0, 6.0, ((0, 32),))
    cotangent = scatter_about(splits[3], (TOKENS, WIDTH), 1.0, 6.0, ((0, 32),))
    neighbours = draw_neighbours(jax.random.fold_in(splits[6], 71), 0)
    counts = draw_counts(jax.random.fold_in(splits[6], 71), 0)
    return dict(queries=queries, key_rows=key_rows, value_rows=value_rows, cotangent=cotangent, neighbours=neighbours, counts=counts)


def attend_tile(q_tile, g_tile, key_tiles, value_tiles, valid):
    scale = HEAD_DIM ** -0.5
    q_wide = q_tile.astype(jnp.float32)
    g_wide = g_tile.astype(jnp.float32)
    key_wide = key_tiles.astype(jnp.float32)
    value_wide = value_tiles.astype(jnp.float32)
    scores = jnp.einsum("qhd,nkhd->hqnk", q_wide, key_wide) * scale
    scores = jnp.where(valid[None, None, :, None], scores, -jnp.inf)
    highest = jnp.max(scores, axis=(2, 3), keepdims=True)
    raised = jnp.exp(scores - highest)
    totals = jnp.sum(raised, axis=(2, 3), keepdims=True)
    weights = raised / totals
    weights_low = weights.astype(jnp.bfloat16).astype(jnp.float32)
    attended = jnp.einsum("hqnk,nkhd->qhd", weights_low, value_wide).astype(jnp.bfloat16)
    inner = jnp.sum(g_wide * attended.astype(jnp.float32), axis=2).T
    grad_weights = jnp.einsum("qhd,nkhd->hqnk", g_wide, value_wide)
    grad_scores = weights * (grad_weights - inner[:, :, None, None])
    grad_low = grad_scores.astype(jnp.bfloat16).astype(jnp.float32)
    grad_query = (scale * jnp.einsum("hqnk,nkhd->qhd", grad_low, key_wide)).astype(jnp.bfloat16)
    key_part = scale * jnp.einsum("hqnk,qhd->nkhd", grad_low, q_wide)
    value_part = jnp.einsum("hqnk,qhd->nkhd", weights_low, g_wide)
    return attended, grad_query, key_part, value_part


def reference(queries, key_rows, value_rows, cotangent, neighbours, counts):
    width = HEADS * HEAD_DIM
    tile_shape = (NBLK, BLOCK, HEADS, HEAD_DIM)
    key_tiles = key_rows.reshape(tile_shape)
    value_tiles = value_rows.reshape(tile_shape)
    slot_index = jnp.arange(NB, dtype=jnp.int32)
    zero_grads = jnp.zeros(tile_shape, jnp.float32)

    def visit(running, inputs):
        grad_k, grad_v = running
        q_tile, g_tile, tile_ids, tile_count = inputs
        outcome = attend_tile(q_tile, g_tile, key_tiles[tile_ids], value_tiles[tile_ids], slot_index < tile_count)
        grad_k = grad_k.at[tile_ids].add(outcome[2])
        grad_v = grad_v.at[tile_ids].add(outcome[3])
        return (grad_k, grad_v), (outcome[0], outcome[1])

    (grad_k, grad_v), (attended, grad_query) = lax.scan(
        visit, (zero_grads, zero_grads),
        (queries.reshape(tile_shape), cotangent.reshape(tile_shape), neighbours, counts))
    return (attended.reshape(TOKENS, width),
            grad_query.reshape(TOKENS, width),
            grad_k.reshape(TOKENS, width).astype(jnp.bfloat16),
            grad_v.reshape(TOKENS, width).astype(jnp.bfloat16))
```

```python
import functools

import jax
import jax.numpy as jnp
from jax import lax
from jax.experimental import pallas as pl
from jax.experimental.pallas import tpu as pltpu
from jax.sharding import PartitionSpec as P

HEAD_DIM = 128
BLOCK = 128
MESH = pl.DeviceIdType.MESH
BF16 = jnp.bfloat16
F32 = jnp.float32
NT = (((1,), (1,)), ((), ()))


def place(seqs, heads):
    seq, head = lax.axis_index("seq"), lax.axis_index("head")
    return seq // 2, lax.rem(seq, 2) * heads + head, seqs // 2


def member(group, rank, heads):
    return (group * 2 + rank // heads, lax.rem(rank, heads))


def greet(seqs, heads):
    group, rank, groups = place(seqs, heads)
    size = 2 * heads
    barrier = pltpu.get_barrier_semaphore()
    targets = [member(group, lax.rem(rank + k, size), heads) for k in range(1, size)]
    targets += [member(lax.rem(group + d, groups), rank, heads) for d in (1, groups - 1)]
    for target in targets:
        pl.semaphore_signal(barrier, inc=1, device_id=target, device_id_type=MESH)
    pl.semaphore_wait(barrier, len(targets))


def gather_kernel(seqs, heads, *refs):
    sources, wins, (s1, r1, s2, r2, own_sem) = refs[:4], refs[4:8], refs[8:]
    group, rank, groups = place(seqs, heads)
    size = 2 * heads
    tok, cols = sources[0].shape[0], sources[0].shape[1] // size
    greet(seqs, heads)

    def here(a, piece):
        return pl.ds(pl.multiple_of((piece + (heads if a < 2 else 0)) * tok, tok), tok)

    def columns(r):
        return pl.ds(pl.multiple_of(r * cols, cols), cols)

    first, own = {}, []
    for a in range(4):
        copy = pltpu.make_async_copy(
            sources[a].at[:, columns(rank)], wins[a].at[here(a, rank), :], own_sem.at[a]
        )
        copy.start()
        own.append(copy)
        for k in range(1, size):
            peer = lax.rem(rank + k, size)
            copy = pltpu.make_async_remote_copy(
                src_ref=sources[a].at[:, columns(peer)],
                dst_ref=wins[a].at[here(a, rank), :],
                send_sem=s1.at[a, k],
                recv_sem=r1.at[a, k],
                device_id=member(group, peer, heads),
                device_id_type=MESH,
            )
            copy.start()
            first[a, k] = copy
    second = []
    for a in range(2):
        for k in range(size):
            if k == 0:
                own[a].wait()
            else:
                first[a, k].wait_recv()
            piece = lax.rem(rank - k + size, size)
            other = lax.rem(group + 2 * (piece // heads) - 1 + groups, groups)
            row = lax.rem(piece + 3 * heads, 4 * heads)
            copy = pltpu.make_async_remote_copy(
                src_ref=wins[a].at[here(a, piece), :],
                dst_ref=wins[a].at[pl.ds(pl.multiple_of(row * tok, tok), tok), :],
                send_sem=s2.at[a, k],
                recv_sem=r2.at[a, k],
                device_id=member(other, rank, heads),
                device_id_type=MESH,
            )
            copy.start()
            second.append(copy)
    for a in range(2, 4):
        own[a].wait()
        for k in range(1, size):
            first[a, k].wait_recv()
    for copy in first.values():
        copy.wait_send()
    for copy in second:
        copy.wait()


def attend_kernel(ids, used, q_ref, g_ref, k_ref, v_ref, o_ref, dq_ref, dk_ref, dv_ref, kt, vt, dk, dv):
    b = pl.program_id(1)
    slots = ids.shape[1]
    scale = HEAD_DIM**-0.5

    @pl.when(b == 0)
    def _():
        dk[...] = jnp.zeros_like(dk)
        dv[...] = jnp.zeros_like(dv)
        kt[...] = k_ref[...].T
        vt[...] = v_ref[...].T

    count = used[b]

    def visit(n):
        rows = [pl.ds(pl.multiple_of(ids[b, i] * BLOCK, BLOCK), BLOCK) for i in range(n)]
        q, g = q_ref[...], g_ref[...]
        keys = jnp.concatenate([k_ref[r, :] for r in rows], 0)
        values = jnp.concatenate([v_ref[r, :] for r in rows], 0)
        scores = lax.dot_general(keys, q, NT, preferred_element_type=F32) * scale
        slot = lax.broadcasted_iota(jnp.int32, scores.shape, 0) // BLOCK
        scores = jnp.where(slot < count, scores, -jnp.inf)
        raised = jnp.exp(scores - jnp.max(scores, axis=0, keepdims=True))
        weights = raised * (1.0 / jnp.sum(raised, axis=0, keepdims=True))
        low = weights.astype(BF16)
        vgt = jnp.concatenate([vt[:, r] for r in rows], 1)
        out = jnp.dot(vgt, low, preferred_element_type=F32).astype(BF16).astype(F32)
        o_ref[...] = out.T.astype(BF16)
        inner = jnp.sum(out * g.astype(F32).T, axis=0, keepdims=True)
        grad = lax.dot_general(values, g, NT, preferred_element_type=F32)
        grad_low = (weights * (grad - inner)).astype(BF16)
        kgt = jnp.concatenate([kt[:, r] for r in rows], 1)
        dqt = jnp.dot(kgt, grad_low, preferred_element_type=F32) * scale
        dq_ref[...] = dqt.T.astype(BF16)
        part_k = jnp.dot(grad_low, q, preferred_element_type=F32)
        part_v = jnp.dot(low, g, preferred_element_type=F32)
        for i, r in enumerate(rows):
            dk[r, :] += part_k[i * BLOCK : (i + 1) * BLOCK]
            dv[r, :] += part_v[i * BLOCK : (i + 1) * BLOCK]

    for n in range(2, slots + 1, 2):
        pl.when((count <= n) & (count > n - 2))(functools.partial(visit, n))

    @pl.when(b == pl.num_programs(1) - 1)
    def _():
        dk_ref[...] = (dk[...] * scale).astype(BF16)
        dv_ref[...] = dv[...].astype(BF16)


def return_kernel(seqs, heads, *refs):
    (att, gq, gk, gv), outs = refs[:4], refs[4:8]
    halo, mine, s1, r1, s2, r2, own_sem, load_sem = refs[8:]
    group, rank, groups = place(seqs, heads)
    size = 2 * heads
    tok, cols = outs[0].shape[0], outs[0].shape[1] // size
    greet(seqs, heads)

    def rows(r):
        return pl.ds(pl.multiple_of(r * tok, tok), tok)

    to = pl.ds(pl.multiple_of(rank * cols, cols), cols)
    halos, loads, sent, own = {}, [], [], []
    for a, grad in enumerate((gk, gv)):
        load = pltpu.make_async_copy(
            grad.at[pl.ds(heads * tok, size * tok), :], mine.at[a], load_sem.at[a]
        )
        load.start()
        loads.append(load)
        for k in range(size):
            piece = lax.rem(rank + k, size)
            other = lax.rem(group + 1 - 2 * (piece // heads) + groups, groups)
            copy = pltpu.make_async_remote_copy(
                src_ref=grad.at[rows(lax.rem(piece + 3 * heads, 4 * heads)), :],
                dst_ref=halo.at[a, rows(piece), :],
                send_sem=s1.at[a, k],
                recv_sem=r1.at[a, k],
                device_id=member(other, rank, heads),
                device_id_type=MESH,
            )
            copy.start()
            halos[a, k] = copy

    def hand_over(a, k, source):
        peer = lax.rem(rank + k, size)
        if k == 0:
            copy = pltpu.make_async_copy(source, outs[a].at[:, to], own_sem.at[a])
            own.append(copy)
        else:
            copy = pltpu.make_async_remote_copy(
                src_ref=source,
                dst_ref=outs[a].at[:, to],
                send_sem=s2.at[a, k],
                recv_sem=r2.at[a, k],
                device_id=member(group, peer, heads),
                device_id_type=MESH,
            )
            sent.append(copy)
        copy.start()

    for a, value in enumerate((att, gq)):
        for k in range(size):
            hand_over(a, k, value.at[rows(lax.rem(rank + k, size)), :])
    for a in range(2):
        loads[a].wait()
        for k in range(size):
            halos[a, k].wait_recv()
            piece = rows(lax.rem(rank + k, size))
            total = mine[a, piece, :].astype(F32) + halo[a, piece, :].astype(F32)
            mine[a, piece, :] = total.astype(BF16)
            hand_over(a + 2, k, mine.at[a, piece, :])
    for copy in halos.values():
        copy.wait_send()
    for copy in sent + own:
        copy.wait()


def local(seqs, heads, queries, key_rows, value_rows, cotangent, neighbours, counts):
    tok, width = queries.shape
    size = 2 * heads
    cols = width // size
    inner, window = size * tok, 2 * size * tok
    blocks = inner // BLOCK
    anywhere = pl.BlockSpec(memory_space=pl.ANY)
    dma = pltpu.SemaphoreType.DMA

    kw, vw, qw, gw = pl.pallas_call(
        functools.partial(gather_kernel, seqs, heads),
        out_shape=[jax.ShapeDtypeStruct((n, cols), BF16) for n in (window, window, inner, inner)],
        in_specs=[anywhere] * 4,
        out_specs=[anywhere] * 4,
        scratch_shapes=[dma((4, size)), dma((4, size)), dma((2, size)), dma((2, size)), dma((4,))],
        compiler_params=pltpu.CompilerParams(collective_id=0, has_side_effects=True),
        name="gather",
    )(key_rows, value_rows, queries, cotangent)

    first = lax.axis_index("seq") // 2 * blocks
    total = neighbours.shape[0]
    ids = lax.dynamic_slice_in_dim(neighbours, first, blocks, 0)
    ids = (ids - first + blocks // 2) % total
    used = lax.dynamic_slice_in_dim(counts, first, blocks, 0)
    tile = pl.BlockSpec((BLOCK, HEAD_DIM), lambda c, b, *_: (b, c))
    whole = pl.BlockSpec((window, HEAD_DIM), lambda c, b, *_: (0, c))
    att, gq, gk, gv = pl.pallas_call(
        attend_kernel,
        out_shape=[jax.ShapeDtypeStruct((n, cols), BF16) for n in (inner, inner, window, window)],
        grid_spec=pltpu.PrefetchScalarGridSpec(
            num_scalar_prefetch=2,
            grid=(cols // HEAD_DIM, blocks),
            in_specs=[tile, tile, whole, whole],
            out_specs=[tile, tile, whole, whole],
            scratch_shapes=[
                pltpu.VMEM((HEAD_DIM, window), BF16),
                pltpu.VMEM((HEAD_DIM, window), BF16),
                pltpu.VMEM((window, HEAD_DIM), F32),
                pltpu.VMEM((window, HEAD_DIM), F32),
            ],
        ),
        compiler_params=pltpu.CompilerParams(vmem_limit_bytes=50 * 2**20),
        name="attend",
    )(ids, used, qw, gw, kw, vw)

    return pl.pallas_call(
        functools.partial(return_kernel, seqs, heads),
        out_shape=[jax.ShapeDtypeStruct((tok, width), BF16)] * 4,
        in_specs=[anywhere] * 4,
        out_specs=[anywhere] * 4,
        scratch_shapes=[
            pltpu.VMEM((2, inner, cols), BF16),
            pltpu.VMEM((2, inner, cols), BF16),
            dma((2, size)),
            dma((2, size)),
            dma((4, size)),
            dma((4, size)),
            dma((4,)),
            dma((2,)),
        ],
        compiler_params=pltpu.CompilerParams(
            collective_id=1, has_side_effects=True, vmem_limit_bytes=50 * 2**20
        ),
        name="give_back",
    )(att, gq, gk, gv)


def solution(mesh):
    rows = P(("seq", "head"), None)
    return jax.shard_map(
        functools.partial(local, mesh.shape["seq"], mesh.shape["head"]),
        mesh=mesh,
        in_specs=(rows, rows, rows, rows, P(), P()),
        out_specs=(rows,) * 4,
        check_vma=False,
    )
```

```python
import functools

import jax
import jax.numpy as jnp
from jax import lax
from jax.experimental import pallas as pl
from jax.experimental.pallas import tpu as pltpu
from jax.sharding import PartitionSpec as P

HEAD_DIM = 128
BLOCK = 128
MESH = pl.DeviceIdType.MESH
BF16 = jnp.bfloat16
F32 = jnp.float32
NT = (((1,), (1,)), ((), ()))


def place(seqs, heads):
    seq, head = lax.axis_index("seq"), lax.axis_index("head")
    return seq // 2, lax.rem(seq, 2) * heads + head, seqs // 2


def member(group, rank, heads):
    return (group * 2 + rank // heads, lax.rem(rank, heads))


def greet(seqs, heads):
    group, rank, groups = place(seqs, heads)
    size = 2 * heads
    barrier = pltpu.get_barrier_semaphore()
    targets = [member(group, lax.rem(rank + k, size), heads) for k in range(1, size)]
    targets += [member(lax.rem(group + d, groups), rank, heads) for d in (1, groups - 1)]
    for target in targets:
        pl.semaphore_signal(barrier, inc=1, device_id=target, device_id_type=MESH)
    pl.semaphore_wait(barrier, len(targets))


def layer_kernel(seqs, heads, ids, used, named, *refs):
    sources, outs = refs[:4], refs[4:8]
    kv, qs, gs, kvw, kvt, part, att, gq, grads, halo = refs[8:18]
    s1, r1, own1, s2, r2, s3, r3, s4, r4, own4 = refs[18:]
    group, rank, groups = place(seqs, heads)
    size = 2 * heads
    tok = sources[0].shape[0]
    planes, window = kv.shape[0], kv.shape[1] // BLOCK
    blocks = window // 2
    slots = ids.shape[0] // blocks
    cols = planes * HEAD_DIM
    per = -(-2 * size // blocks)
    scale = HEAD_DIM**-0.5
    low_lanes, high_lanes = pl.ds(0, HEAD_DIM), pl.ds(HEAD_DIM, HEAD_DIM)

    def rows(r):
        return pl.ds(pl.multiple_of(r * tok, tok), tok)

    def columns(r, c):
        return pl.ds(pl.multiple_of(r * cols + c * HEAD_DIM, HEAD_DIM), HEAD_DIM)

    def copy_to(source, target, sends, receives, device):
        return pltpu.make_async_remote_copy(
            src_ref=source,
            dst_ref=target,
            send_sem=sends,
            recv_sem=receives,
            device_id=device,
            device_id_type=MESH,
        )

    def first(c, a, k):
        peer = lax.rem(rank + k, size)
        source = sources[a].at[:, columns(peer, c)]
        if a < 2:
            target = kv.at[c, rows(rank + heads), (low_lanes, high_lanes)[a]]
        else:
            target = (qs, gs)[a - 2].at[c, rows(rank), :]
        if k == 0:
            return pltpu.make_async_copy(source, target, own1.at[c, a])
        return copy_to(source, target, s1.at[c, a, k], r1.at[c, a, k], member(group, peer, heads))

    def arrive(copy, k):
        if k == 0:
            copy.wait()
        else:
            copy.wait_recv()

    def second(c, k):
        piece = lax.rem(rank - k + size, size)
        other = lax.rem(group + 2 * (piece // heads) - 1 + groups, groups)
        return copy_to(
            kv.at[c, rows(piece + heads), :],
            kv.at[c, rows(lax.rem(piece + 3 * heads, 4 * heads)), :],
            s2.at[c, k],
            r2.at[c, k],
            member(other, rank, heads),
        )

    def forward(c, k):
        arrive(first(c, 0, k), k)
        arrive(first(c, 1, k), k)
        second(c, k).start()

    def third(c, k):
        piece = lax.rem(rank + k, size)
        other = lax.rem(group + 1 - 2 * (piece // heads) + groups, groups)
        return copy_to(
            grads.at[c, rows(lax.rem(piece + 3 * heads, 4 * heads)), :],
            halo.at[c, rows(piece), :],
            s3.at[c, k],
            r3.at[c, k],
            member(other, rank, heads),
        )

    def fourth(c, a, k):
        peer = lax.rem(rank + k, size)
        if a < 2:
            source = (att, gq)[a].at[c, rows(peer), :]
        else:
            source = grads.at[c, rows(peer + heads), (low_lanes, high_lanes)[a - 2]]
        target = outs[a].at[:, columns(rank, c)]
        if k == 0:
            return pltpu.make_async_copy(source, target, own4.at[c, a])
        return copy_to(source, target, s4.at[c, a, k], r4.at[c, a, k], member(group, peer, heads))

    def settle(c, k):
        third(c, k).wait_recv()
        piece = lax.rem(rank + k, size)
        mine = rows(piece + heads)
        total = grads[c, mine, :].astype(F32) + halo[c, rows(piece), :].astype(F32)
        grads[c, mine, :] = total.astype(BF16)
        fourth(c, 2, k).start()
        fourth(c, 3, k).start()

    greet(seqs, heads)

    def begin(c, _):
        for a in range(4):
            for k in range(size):
                first(c, a, k).start()
        return 0

    lax.fori_loop(0, planes, begin, 0)
    part[blocks * slots] = jnp.zeros(part.shape[1:], F32)
    for k in range(size):
        forward(0, k)

    def attend(c, b):
        picks = [ids[b * slots + i] for i in range(slots)]
        here = pl.ds(pl.multiple_of(b * BLOCK, BLOCK), BLOCK)
        q, g = qs[c, here, :], gs[c, here, :]
        none = jnp.zeros_like(q)
        both = jnp.concatenate(
            [jnp.concatenate([q, none], 1), jnp.concatenate([none, g], 1)], 0
        )
        tiles = jnp.concatenate([kvw[p] for p in picks], 0)
        product = lax.dot_general(tiles, both, NT, preferred_element_type=F32)
        slot = lax.broadcasted_iota(jnp.int32, (slots * BLOCK, HEAD_DIM), 0) // BLOCK
        scores = jnp.where(slot < used[b], product[:, :HEAD_DIM] * scale, -jnp.inf)
        raised = jnp.exp(scores - jnp.max(scores, axis=0, keepdims=True))
        weights = raised * (1.0 / jnp.sum(raised, axis=0, keepdims=True))
        low = weights.astype(BF16)
        vgt = jnp.concatenate([kvt[p, high_lanes, :] for p in picks], 1)
        out = jnp.dot(vgt, low, preferred_element_type=F32).astype(BF16).astype(F32)
        att[c, here, :] = out.T.astype(BF16)
        inner = jnp.sum(out * g.astype(F32).T, axis=0, keepdims=True)
        grad_low = (weights * (product[:, HEAD_DIM:] - inner)).astype(BF16)
        kgt = jnp.concatenate([kvt[p, low_lanes, :] for p in picks], 1)
        dqt = jnp.dot(kgt, grad_low, preferred_element_type=F32) * scale
        gq[c, here, :] = dqt.T.astype(BF16)
        pair = jnp.concatenate([grad_low, low], 1)
        sums = jnp.dot(pair, both, preferred_element_type=F32)
        part[pl.ds(b * slots, slots)] = sums.reshape((slots, BLOCK, 2 * HEAD_DIM))

    def plane(c, _):
        for k in range(size):
            second(c, k).wait_recv()
            for a in (2, 3):
                arrive(first(c, a, k), k)

        def prepare(w, _):
            tile = kv[c, pl.ds(pl.multiple_of(w * BLOCK, BLOCK), BLOCK), :]
            kvw[w] = tile
            kvt[w] = tile.T
            return 0

        lax.fori_loop(0, window, prepare, 0)

        def step(b, _):
            for k in range(size):
                pl.when((b == k // per) & (c + 1 < planes))(functools.partial(forward, c + 1, k))
                pl.when((b == blocks // 2 + k // per) & (c > 0))(
                    functools.partial(settle, c - 1, k)
                )
            attend(c, b)
            return 0

        lax.fori_loop(0, blocks, step, 0)

        def collect(w, _):
            def add(b, total):
                return total + part[named[w * blocks + b]]

            total = lax.fori_loop(
                jnp.maximum(0, w - blocks),
                jnp.minimum(blocks - 1, w) + 1,
                add,
                jnp.zeros((BLOCK, 2 * HEAD_DIM), F32),
            )
            lane = lax.broadcasted_iota(jnp.int32, total.shape, 1)
            total = total * jnp.where(lane < HEAD_DIM, scale, 1.0)
            grads[c, pl.ds(pl.multiple_of(w * BLOCK, BLOCK), BLOCK), :] = total.astype(BF16)
            return 0

        lax.fori_loop(0, window, collect, 0)
        for k in range(size):
            third(c, k).start()
        for k in range(size):
            for a in range(2):
                fourth(c, a, k).start()
        return 0

    lax.fori_loop(0, planes, plane, 0)
    for k in range(size):
        settle(planes - 1, k)

    def finish(c, _):
        for k in range(size):
            second(c, k).wait_send()
            third(c, k).wait_send()
            for a in range(4):
                if k:
                    first(c, a, k).wait_send()
                fourth(c, a, k).wait()
        return 0

    lax.fori_loop(0, planes, finish, 0)


def local(seqs, heads, queries, key_rows, value_rows, cotangent, neighbours, counts):
    tok, width = queries.shape
    size = 2 * heads
    planes = width // size // HEAD_DIM
    inner, window = size * tok, 2 * size * tok
    blocks = inner // BLOCK
    slots = neighbours.shape[1]
    anywhere = pl.BlockSpec(memory_space=pl.ANY)
    scalars = pl.BlockSpec(memory_space=pltpu.SMEM)
    dma = pltpu.SemaphoreType.DMA

    start = lax.axis_index("seq") // 2 * blocks
    ids = lax.dynamic_slice_in_dim(neighbours, start, blocks, 0)
    ids = (ids - start + blocks // 2) % neighbours.shape[0]
    used = lax.dynamic_slice_in_dim(counts, start, blocks, 0)
    slot = jnp.arange(slots, dtype=jnp.int32)
    entry = jnp.arange(blocks, dtype=jnp.int32)[:, None] * slots + slot[None, :]
    match = ids[None] == jnp.arange(2 * blocks, dtype=jnp.int32)[:, None, None]
    match = match & (slot[None, :] < used[:, None])[None]
    named = jnp.min(jnp.where(match, entry[None], blocks * slots), axis=2)

    return pl.pallas_call(
        functools.partial(layer_kernel, seqs, heads),
        out_shape=[jax.ShapeDtypeStruct((tok, width), BF16)] * 4,
        in_specs=[scalars] * 3 + [anywhere] * 4,
        out_specs=[anywhere] * 4,
        scratch_shapes=[
            pltpu.VMEM((planes, window, 2 * HEAD_DIM), BF16),
            pltpu.VMEM((planes, inner, HEAD_DIM), BF16),
            pltpu.VMEM((planes, inner, HEAD_DIM), BF16),
            pltpu.VMEM((2 * blocks, BLOCK, 2 * HEAD_DIM), BF16),
            pltpu.VMEM((2 * blocks, 2 * HEAD_DIM, BLOCK), BF16),
            pltpu.VMEM((blocks * slots + 1, BLOCK, 2 * HEAD_DIM), F32),
            pltpu.VMEM((planes, inner, HEAD_DIM), BF16),
            pltpu.VMEM((planes, inner, HEAD_DIM), BF16),
            pltpu.VMEM((planes, window, 2 * HEAD_DIM), BF16),
            pltpu.VMEM((planes, inner, 2 * HEAD_DIM), BF16),
            dma((planes, 4, size)),
            dma((planes, 4, size)),
            dma((planes, 4)),
            dma((planes, size)),
            dma((planes, size)),
            dma((planes, size)),
            dma((planes, size)),
            dma((planes, 4, size)),
            dma((planes, 4, size)),
            dma((planes, 4)),
        ],
        compiler_params=pltpu.CompilerParams(
            collective_id=0, has_side_effects=True, vmem_limit_bytes=60 * 2**20
        ),
        name="layer",
    )(
        ids.reshape(-1),
        used,
        named.reshape(-1),
        key_rows,
        value_rows,
        queries,
        cotangent,
    )


def solution(mesh):
    rows = P(("seq", "head"), None)
    return jax.shard_map(
        functools.partial(local, mesh.shape["seq"], mesh.shape["head"]),
        mesh=mesh,
        in_specs=(rows, rows, rows, rows, P(), P()),
        out_specs=(rows,) * 4,
        check_vma=False,
    )
```

```python
import functools

import jax
import jax.numpy as jnp
from jax import lax
from jax.experimental import pallas as pl
from jax.experimental.pallas import tpu as pltpu
from jax.sharding import PartitionSpec as P

HEAD_DIM = 128
BLOCK = 128
MESH = pl.DeviceIdType.MESH
BF16 = jnp.bfloat16
F32 = jnp.float32
NT = (((1,), (1,)), ((), ()))


def place(seqs, heads):
    seq, head = lax.axis_index("seq"), lax.axis_index("head")
    return seq // 2, lax.rem(seq, 2) * heads + head, seqs // 2


def member(group, rank, heads):
    return (group * 2 + rank // heads, lax.rem(rank, heads))


def greet(seqs, heads):
    group, rank, groups = place(seqs, heads)
    size = 2 * heads
    barrier = pltpu.get_barrier_semaphore()
    targets = [member(group, lax.rem(rank + k, size), heads) for k in range(1, size)]
    targets += [member(lax.rem(group + d, groups), rank, heads) for d in (1, groups - 1)]
    for target in targets:
        pl.semaphore_signal(barrier, inc=1, device_id=target, device_id_type=MESH)
    pl.semaphore_wait(barrier, len(targets))


def layer_kernel(seqs, heads, ids, used, named, *refs):
    sources, outs = refs[:4], refs[4:8]
    kv, qs, gs, kvw, kvt, part, att, gq, grads, halo = refs[8:18]
    s1, r1, own1, s2, r2, s3, r3, s4, r4, own4 = refs[18:]
    group, rank, groups = place(seqs, heads)
    size = 2 * heads
    tok = sources[0].shape[0]
    planes, window = kv.shape[0], kv.shape[1] // BLOCK
    blocks = window // 2
    slots = ids.shape[0] // blocks
    cols = planes * HEAD_DIM
    per = -(-2 * size // blocks)
    scale = HEAD_DIM**-0.5
    low_lanes, high_lanes = pl.ds(0, HEAD_DIM), pl.ds(HEAD_DIM, HEAD_DIM)

    def rows(r):
        return pl.ds(pl.multiple_of(r * tok, tok), tok)

    def columns(r, c):
        return pl.ds(pl.multiple_of(r * cols + c * HEAD_DIM, HEAD_DIM), HEAD_DIM)

    def copy_to(source, target, sends, receives, device):
        return pltpu.make_async_remote_copy(
            src_ref=source,
            dst_ref=target,
            send_sem=sends,
            recv_sem=receives,
            device_id=device,
            device_id_type=MESH,
        )

    def first(c, a, k):
        peer = lax.rem(rank + k, size)
        source = sources[a].at[:, columns(peer, c)]
        if a < 2:
            target = kv.at[c, rows(rank + heads), (low_lanes, high_lanes)[a]]
        else:
            target = (qs, gs)[a - 2].at[c, rows(rank), :]
        if k == 0:
            return pltpu.make_async_copy(source, target, own1.at[c, a])
        return copy_to(source, target, s1.at[c, a, k], r1.at[c, a, k], member(group, peer, heads))

    def arrive(copy, k):
        if k == 0:
            copy.wait()
        else:
            copy.wait_recv()

    def second(c, k):
        piece = lax.rem(rank - k + size, size)
        other = lax.rem(group + 2 * (piece // heads) - 1 + groups, groups)
        return copy_to(
            kv.at[c, rows(piece + heads), :],
            kv.at[c, rows(lax.rem(piece + 3 * heads, 4 * heads)), :],
            s2.at[c, k],
            r2.at[c, k],
            member(other, rank, heads),
        )

    def forward(c, k):
        arrive(first(c, 0, k), k)
        arrive(first(c, 1, k), k)
        second(c, k).start()

    def third(c, k):
        piece = lax.rem(rank + k, size)
        other = lax.rem(group + 1 - 2 * (piece // heads) + groups, groups)
        return copy_to(
            grads.at[c, rows(lax.rem(piece + 3 * heads, 4 * heads)), :],
            halo.at[c, rows(piece), :],
            s3.at[c, k],
            r3.at[c, k],
            member(other, rank, heads),
        )

    def fourth(c, a, k):
        peer = lax.rem(rank + k, size)
        if a < 2:
            source = (att, gq)[a].at[c, rows(peer), :]
        else:
            source = grads.at[c, rows(peer + heads), (low_lanes, high_lanes)[a - 2]]
        target = outs[a].at[:, columns(rank, c)]
        if k == 0:
            return pltpu.make_async_copy(source, target, own4.at[c, a])
        return copy_to(source, target, s4.at[c, a, k], r4.at[c, a, k], member(group, peer, heads))

    def settle(c, k):
        third(c, k).wait_recv()
        piece = lax.rem(rank + k, size)
        mine = rows(piece + heads)
        total = grads[c, mine, :].astype(F32) + halo[c, rows(piece), :].astype(F32)
        grads[c, mine, :] = total.astype(BF16)
        fourth(c, 2, k).start()
        fourth(c, 3, k).start()

    greet(seqs, heads)

    def begin(c, _):
        for a in range(4):
            for k in range(size):
                first(c, a, k).start()
        return 0

    lax.fori_loop(0, planes, begin, 0)

    def clear(i, _):
        part[i] = jnp.zeros(part.shape[1:], F32)
        return 0

    lax.fori_loop(0, part.shape[0], clear, 0)

    def lead(c, _):
        forward(c, 0)
        return 0

    lax.fori_loop(0, planes, lead, 0)
    for k in range(1, size):
        forward(0, k)

    def attend(c, b):
        picks = [ids[b * slots + i] for i in range(slots)]
        here = pl.ds(pl.multiple_of(b * BLOCK, BLOCK), BLOCK)
        q, g = qs[c, here, :], gs[c, here, :]
        none = jnp.zeros_like(q)
        both = jnp.concatenate(
            [jnp.concatenate([q, none], 1), jnp.concatenate([none, g], 1)], 0
        )
        tiles = jnp.concatenate([kvw[p] for p in picks], 0)
        product = lax.dot_general(tiles, both, NT, preferred_element_type=F32)
        slot = lax.broadcasted_iota(jnp.int32, (slots * BLOCK, HEAD_DIM), 0) // BLOCK
        scores = jnp.where(slot < used[b], product[:, :HEAD_DIM] * scale, -jnp.inf)
        raised = jnp.exp(scores - jnp.max(scores, axis=0, keepdims=True))
        weights = raised * (1.0 / jnp.sum(raised, axis=0, keepdims=True))
        low = weights.astype(BF16)
        vgt = jnp.concatenate([kvt[p, high_lanes, :] for p in picks], 1)
        out = jnp.dot(vgt, low, preferred_element_type=F32).astype(BF16).astype(F32)
        att[c, here, :] = out.T.astype(BF16)
        inner = jnp.sum(out * g.astype(F32).T, axis=0, keepdims=True)
        grad_low = (weights * (product[:, HEAD_DIM:] - inner)).astype(BF16)
        kgt = jnp.concatenate([kvt[p, low_lanes, :] for p in picks], 1)
        dqt = jnp.dot(kgt, grad_low, preferred_element_type=F32) * scale
        gq[c, here, :] = dqt.T.astype(BF16)
        pair = jnp.concatenate([grad_low, low], 1)
        sums = jnp.dot(pair, both, preferred_element_type=F32)
        part[pl.ds(b * slots, slots)] = sums.reshape((slots, BLOCK, 2 * HEAD_DIM))

    def plane(c, _):
        for k in range(size):
            second(c, k).wait_recv()
            for a in (2, 3):
                arrive(first(c, a, k), k)

        def prepare(w, _):
            tile = kv[c, pl.ds(pl.multiple_of(w * BLOCK, BLOCK), BLOCK), :]
            kvw[w] = tile
            kvt[w] = tile.T
            return 0

        lax.fori_loop(0, window, prepare, 0)

        def step(b, _):
            for k in range(size):
                if k:
                    pl.when((b == k // per) & (c + 1 < planes))(
                        functools.partial(forward, c + 1, k)
                    )
                pl.when((b == blocks // 2 + k // per) & (c > 0))(
                    functools.partial(settle, c - 1, k)
                )
            attend(c, b)
            for k in range(size):
                for a in range(2):
                    ready = (b + 1) * BLOCK == (lax.rem(rank + k, size) + 1) * tok
                    pl.when(ready)(fourth(c, a, k).start)
            return 0

        def collect(w, _):
            def add(b, total):
                return total + part[named[w * blocks + b]]

            total = lax.fori_loop(
                jnp.maximum(0, w - blocks),
                jnp.minimum(blocks - 1, w) + 1,
                add,
                jnp.zeros((BLOCK, 2 * HEAD_DIM), F32),
            )
            lane = lax.broadcasted_iota(jnp.int32, total.shape, 1)
            total = total * jnp.where(lane < HEAD_DIM, scale, 1.0)
            grads[c, pl.ds(pl.multiple_of(w * BLOCK, BLOCK), BLOCK), :] = total.astype(BF16)
            return 0

        half = blocks // 2
        lax.fori_loop(0, half, step, 0)
        lax.fori_loop(0, half, collect, 0)
        for k in range(size):
            pl.when(lax.rem(rank + k, size) >= heads)(third(c, k).start)
        lax.fori_loop(half, blocks, step, 0)
        lax.fori_loop(blocks + half, window, collect, 0)
        for k in range(size):
            pl.when(lax.rem(rank + k, size) < heads)(third(c, k).start)
        lax.fori_loop(half, blocks + half, collect, 0)
        return 0

    lax.fori_loop(0, planes, plane, 0)
    for k in range(size):
        settle(planes - 1, k)

    def finish(c, _):
        for k in range(size):
            second(c, k).wait_send()
            third(c, k).wait_send()
            for a in range(4):
                if k:
                    first(c, a, k).wait_send()
                fourth(c, a, k).wait()
        return 0

    lax.fori_loop(0, planes, finish, 0)


def local(seqs, heads, queries, key_rows, value_rows, cotangent, neighbours, counts):
    tok, width = queries.shape
    size = 2 * heads
    planes = width // size // HEAD_DIM
    inner, window = size * tok, 2 * size * tok
    blocks = inner // BLOCK
    slots = neighbours.shape[1]
    anywhere = pl.BlockSpec(memory_space=pl.ANY)
    scalars = pl.BlockSpec(memory_space=pltpu.SMEM)
    dma = pltpu.SemaphoreType.DMA

    start = lax.axis_index("seq") // 2 * blocks
    ids = lax.dynamic_slice_in_dim(neighbours, start, blocks, 0)
    ids = (ids - start + blocks // 2) % neighbours.shape[0]
    used = lax.dynamic_slice_in_dim(counts, start, blocks, 0)
    slot = jnp.arange(slots, dtype=jnp.int32)
    entry = jnp.arange(blocks, dtype=jnp.int32)[:, None] * slots + slot[None, :]
    match = ids[None] == jnp.arange(2 * blocks, dtype=jnp.int32)[:, None, None]
    match = match & (slot[None, :] < used[:, None])[None]
    named = jnp.min(jnp.where(match, entry[None], blocks * slots), axis=2)

    return pl.pallas_call(
        functools.partial(layer_kernel, seqs, heads),
        out_shape=[jax.ShapeDtypeStruct((tok, width), BF16)] * 4,
        in_specs=[scalars] * 3 + [anywhere] * 4,
        out_specs=[anywhere] * 4,
        scratch_shapes=[
            pltpu.VMEM((planes, window, 2 * HEAD_DIM), BF16),
            pltpu.VMEM((planes, inner, HEAD_DIM), BF16),
            pltpu.VMEM((planes, inner, HEAD_DIM), BF16),
            pltpu.VMEM((2 * blocks, BLOCK, 2 * HEAD_DIM), BF16),
            pltpu.VMEM((2 * blocks, 2 * HEAD_DIM, BLOCK), BF16),
            pltpu.VMEM((blocks * slots + 1, BLOCK, 2 * HEAD_DIM), F32),
            pltpu.VMEM((planes, inner, HEAD_DIM), BF16),
            pltpu.VMEM((planes, inner, HEAD_DIM), BF16),
            pltpu.VMEM((planes, window, 2 * HEAD_DIM), BF16),
            pltpu.VMEM((planes, inner, 2 * HEAD_DIM), BF16),
            dma((planes, 4, size)),
            dma((planes, 4, size)),
            dma((planes, 4)),
            dma((planes, size)),
            dma((planes, size)),
            dma((planes, size)),
            dma((planes, size)),
            dma((planes, 4, size)),
            dma((planes, 4, size)),
            dma((planes, 4)),
        ],
        compiler_params=pltpu.CompilerParams(
            collective_id=0, has_side_effects=True, vmem_limit_bytes=60 * 2**20
        ),
        name="layer",
    )(
        ids.reshape(-1),
        used,
        named.reshape(-1),
        key_rows,
        value_rows,
        queries,
        cotangent,
    )


def solution(mesh):
    rows = P(("seq", "head"), None)
    return jax.shard_map(
        functools.partial(local, mesh.shape["seq"], mesh.shape["head"]),
        mesh=mesh,
        in_specs=(rows, rows, rows, rows, P(), P()),
        out_specs=(rows,) * 4,
        check_vma=False,
    )
```
